32 devices in a mesh: clip: 2 (over y), frame: 4 (over z), track: 4 (over x, core).
Axes of the slice: x: 2, y: 2, z: 4, core: 2. Of those that a mesh axis runs over, the one named last changes fastest.
Arguments:
- feature_maps: bfloat16 [8, 4096, 256], P(('clip', 'frame')), parts along dimension 0, may hold values from -6 to 6
- query_frame: int32 [1024], P('clip'), parts along dimension 0, may hold values from 0 to 3
- query_row: int32 [1024], P('clip'), parts along dimension 0, may hold values from 0 to 63
- query_col: int32 [1024], P('clip'), parts along dimension 0, may hold values from 0 to 63
- track_order: int32 [1024], P('clip'), parts along dimension 0, may hold values from 0 to 511, each once
- conv_weight: float32 [16, 9], replicated, may hold values from -2 to 2
- conv_bias: float32 [16], replicated, may hold values from -2 to 2
- head_weight: float32 [16], replicated, may hold values from -2 to 2
- mix_in: bfloat16 [256, 1024], replicated, may hold values from -0.375 to 0.375
- temporal_taps: float32 [3, 1024], replicated, may hold values from -2.5 to 2.5
- mix_gain: float32 [1024], replicated, may hold values from 0.25 to 1.75
- mix_out: bfloat16 [1024, 3], replicated, may hold values from -0.1875 to 0.1875
Outputs:
- estimates: float32 [1024, 3, 4], P(('clip', 'frame', 'track')), parts along dimension 0
The draws below stay inside these ranges and needn't reach their ends.
There are 2 independent parts, one for each index of `clip`. The reference program is written for one: setup_inputs(seed, part) draws one part's arguments, and reference() takes and returns one part's arrays. A program takes and returns all parts, laid end to end along the dimension named above; an argument that names none is the same for every part. Nothing has to cross between parts.
Inputs may be any that keep to these rules, and one draw needn't show every extreme that they name: `track_order`: each track appears in exactly one slot.
All inputs are finite; a program needn't handle non-finite values.
Results may differ from the reference program's by a relative error of at most 0.0053.
Values may be sent and summed in bfloat16 or wider, within the bound.
A program may use at most 64 MiB of HBM per device.

```python
import math
import jax
import jax.numpy as jnp
import numpy as np
from jax import lax

CHAN = 256
GRID_H = 64
GRID_W = 64
MIXW = 1024
HID = 16
FRAMES = 4
NTRACK = 512


def place_ends(values, rng, low, high):
    index_at = [jax.random.randint(jax.random.fold_in(rng, axis), (), 0, length) for axis, length in enumerate(values.shape)]
    main_axis = values.shape.index(max(values.shape))
    neighbour = index_at[:main_axis] + [(index_at[main_axis] + 1) % values.shape[main_axis]] + index_at[main_axis + 1:]
    return values.at[tuple(index_at)].set(low).at[tuple(neighbour)].set(high)


def shard_levels(key, dims, pieces, low, top_value):
    def one(axis_at, blocks):
        steps = jax.random.uniform(jax.random.fold_in(jax.random.fold_in(key, 6), axis_at), (blocks,), jnp.float32, low / len(pieces), top_value / len(pieces))
        return jnp.repeat(jnp.exp(steps), dims[axis_at] // blocks).reshape((-1,) + (1,) * (len(dims) - axis_at - 1))

    factor_of = one(*pieces[0])
    for cut in pieces[1:]:
        factor_of = factor_of * one(*cut)
    return factor_of


def cumulative_ranks(number_of, slope):
    loads = [(1 << 20) // math.isqrt(grade ** slope) + 1 for grade in range(1, number_of + 1)]
    scale = 1 + sum(loads) // (1 << 30)
    return np.cumsum(np.array([max(1, weight // scale) for weight in loads]))


def ranked(own_key, extent, amount, slope):
    listing = cumulative_ranks(amount, slope)
    ticket = jax.random.randint(jax.random.fold_in(own_key, 1), extent, 0, int(listing[amount - 1]))
    standing = jnp.searchsorted(jnp.asarray(listing, jnp.int32), ticket, side="right")
    return jax.random.permutation(jax.random.fold_in(own_key, 2), amount)[standing].astype(jnp.int32)


def centred(stream_key, dims, scale, reach, cuts=(), kind=jnp.bfloat16):
    result = jax.random.normal(stream_key, dims, jnp.float32) * scale
    if len(cuts) > 0:
        result = shard_levels(stream_key, dims, cuts, -0.22, 0.18) * result
    return jnp.clip(result, min=-reach, max=reach).astype(kind)


def setup_inputs(seed: int = 0, part: int = 0) -> dict:
    seeds = jax.random.split(jax.random.key(seed), 13)
    part_splits = jax.random.split(jax.random.fold_in(seeds[12], part), 13)
    return {
        "feature_maps": centred(part_splits[0], (FRAMES, GRID_H * GRID_W, CHAN), 1.0, 6.0, ((0, 4),)),
        "query_frame": place_ends(ranked(part_splits[1], (NTRACK,), FRAMES, 2), jax.random.fold_in(part_splits[1], 3), 0, FRAMES - 1).astype(jnp.int32),
        "query_row": place_ends(jax.random.randint(part_splits[2], (NTRACK,), 0, GRID_H), jax.random.fold_in(part_splits[2], 1), 0, GRID_H - 1).astype(jnp.int32),
        "query_col": place_ends(jax.random.randint(part_splits[3], (NTRACK,), 0, GRID_W), jax.random.fold_in(part_splits[3], 1), 0, GRID_W - 1).astype(jnp.int32),
        "track_order": jax.random.permutation(part_splits[4], NTRACK).astype(jnp.int32),
        "conv_weight": centred(seeds[5], (HID, 9), 0.4, 2.0, (), jnp.float32),
        "conv_bias": centred(seeds[6], (HID,), 0.5, 2.0, (), jnp.float32),
        "head_weight": centred(seeds[7], (HID,), 0.5, 2.0, (), jnp.float32),
        "mix_in": centred(seeds[8], (CHAN, MIXW), CHAN ** -0.5, 0.375),
        "temporal_taps": centred(seeds[9], (3, MIXW), 0.6, 2.5, (), jnp.float32),
        "mix_gain": jnp.clip(1.0 + 0.15 * jax.random.normal(seeds[10], (MIXW,), jnp.float32), 0.25, 1.75),
        "mix_out": centred(seeds[11], (MIXW, 3), MIXW ** -0.5, 0.1875),
    }


def conv_logits(cost, conv_weight, conv_bias, head_weight):
    height, width = (cost.shape[1], cost.shape[2])
    padded = jnp.pad(cost, ((0, 0), (1, 1), (1, 1)))
    logit = jnp.zeros(cost.shape, jnp.float32)
    for channel in range(conv_weight.shape[0]):
        acc = jnp.zeros(cost.shape, jnp.float32) + conv_bias[channel]
        for tap in range(9):
            acc = acc + conv_weight[channel, tap] * padded[:, tap // 3:tap // 3 + height, tap % 3:tap % 3 + width]
        logit = logit + head_weight[channel] * jax.nn.relu(acc)
    return logit

def block_terms(qblock, maps, conv_weight, conv_bias, head_weight, row_pos, col_pos):
    cost = lax.dot_general(qblock, maps, (((1,), (1,)), ((), ())), preferred_element_type=jnp.float32)
    cost = cost * (1.0 / math.sqrt(maps.shape[1]))
    logit = conv_logits(cost.reshape(cost.shape[0], GRID_H, GRID_W), conv_weight, conv_bias, head_weight)
    heat = jax.nn.softmax(logit.reshape(cost.shape), axis=-1)
    row_est = lax.optimization_barrier(jnp.sum(heat * row_pos, axis=-1)).astype(jnp.bfloat16)
    col_est = lax.optimization_barrier(jnp.sum(heat * col_pos, axis=-1)).astype(jnp.bfloat16)
    sampled = jnp.dot(heat.astype(jnp.bfloat16), maps, preferred_element_type=jnp.float32).astype(jnp.bfloat16)
    return (sampled, row_est, col_est)

def temporal_mix(extended, temporal_taps, mix_gain, mix_out):
    mixed = temporal_taps[0] * extended[:, :-2] + temporal_taps[1] * extended[:, 1:-1] + temporal_taps[2] * extended[:, 2:]
    normed = mixed * lax.rsqrt(lax.optimization_barrier(jnp.mean(mixed * mixed, axis=-1, keepdims=True)) + 1e-06) * mix_gain
    hidden = jax.nn.gelu(normed).astype(jnp.bfloat16)
    rows, frames_here = (hidden.shape[0], hidden.shape[1])
    delta = jnp.dot(hidden.reshape(rows * frames_here, hidden.shape[2]), mix_out, preferred_element_type=jnp.float32)
    return delta.reshape(rows, frames_here, 3)

def assemble(row_est, col_est, delta):
    return jnp.stack([row_est.astype(jnp.float32) + delta[:, :, 0], col_est.astype(jnp.float32) + delta[:, :, 1], delta[:, :, 2]], axis=1)

def reference(feature_maps, query_frame, query_row, query_col, track_order, conv_weight, conv_bias, head_weight, mix_in, temporal_taps, mix_gain, mix_out):
    pixels = GRID_H * GRID_W
    frame_ids = query_frame[track_order]
    pixel_ids = query_row[track_order] * GRID_W + query_col[track_order]
    flat = (frame_ids * pixels + pixel_ids).astype(jnp.int32)
    queries = feature_maps.reshape(FRAMES * pixels, CHAN)[flat]
    positions = jnp.arange(pixels, dtype=jnp.int32)
    row_pos = (positions // GRID_W).astype(jnp.float32) / (GRID_H - 1)
    col_pos = (positions % GRID_W).astype(jnp.float32) / (GRID_W - 1)
    blk = min(NTRACK, 64)
    blocks = NTRACK // blk

    def per_block(qblock):

        def per_frame(maps):
            return block_terms(qblock, maps, conv_weight, conv_bias, head_weight, row_pos, col_pos)
        return lax.map(per_frame, feature_maps)
    sampled, row_est, col_est = lax.map(per_block, queries.reshape(blocks, blk, CHAN))
    sampled = jnp.transpose(sampled, (0, 2, 1, 3)).reshape(NTRACK, FRAMES, CHAN)
    row_est = jnp.transpose(row_est, (0, 2, 1)).reshape(NTRACK, FRAMES)
    col_est = jnp.transpose(col_est, (0, 2, 1)).reshape(NTRACK, FRAMES)
    projected = jnp.dot(sampled.reshape(NTRACK * FRAMES, CHAN), mix_in, preferred_element_type=jnp.float32)
    projected = projected.reshape(NTRACK, FRAMES, MIXW)
    extended = jnp.pad(projected, ((0, 0), (1, 1), (0, 0)))
    delta = temporal_mix(extended, temporal_taps, mix_gain, mix_out)
    return assemble(row_est, col_est, delta)
```

```python
import functools
import math

import jax
import jax.numpy as jnp
from jax import lax
from jax.experimental import pallas as pl
from jax.experimental.pallas import tpu as pltpu
from jax.sharding import PartitionSpec as P

GRID_H = 64
GRID_W = 64
MESH = pl.DeviceIdType.MESH
LANES = 128
F32 = jnp.float32
BF16 = jnp.bfloat16


def kernel(
    dims,
    *refs,
):
    count = 12
    sources = refs[:count]
    out_ref = refs[count]
    held = refs[count + 1 : 2 * count + 1]
    (
        maps_ref,
        frame_ref,
        row_ref,
        col_ref,
        order_ref,
        weight_ref,
        bias_ref,
        head_ref,
        mix_in_ref,
        taps_ref,
        gain_ref,
        mix_out_ref,
    ) = held
    (
        qpart,
        qrecv,
        xs,
        bands,
        logit,
        ssend,
        srecv,
        qsend_sem,
        qrecv_sem,
        ssend_sem,
        srecv_sem,
        load_sem,
        maps_sem,
    ) = refs[2 * count + 1 :]
    frames, tracks, sub, group, wire = dims
    stages = frames // group
    rows = group * sub
    pixels, chan = maps_ref.shape
    total = order_ref.shape[1]
    slots_here = frames * sub
    hid = weight_ref.shape[0]
    tiles = pixels // LANES
    me = lax.axis_index("frame")
    track_here = lax.axis_index("track")

    barrier = pltpu.get_barrier_semaphore()
    for off in range(1, frames):
        pl.semaphore_signal(
            barrier, inc=1, device_id={"frame": lax.rem(me + off, frames)}, device_id_type=MESH
        )

    pieces = maps_sem.shape[0]
    piece = pixels // pieces
    loads = {}
    for i in (1, 2, 3, 4):
        loads[i] = pltpu.make_async_copy(sources[i], held[i], load_sem.at[i])
        loads[i].start()
    maps_loads = []
    for i in range(pieces):
        part = pl.ds(i * piece, piece)
        copy = pltpu.make_async_copy(sources[0].at[part], maps_ref.at[part], maps_sem.at[i])
        copy.start()
        maps_loads.append(copy)
    for i in (5, 6, 7, 8, 9, 10, 11):
        loads[i] = pltpu.make_async_copy(sources[i], held[i], load_sem.at[i])
        loads[i].start()
    for i in (1, 2, 3, 4):
        loads[i].wait()

    code = (frame_ref[...] * pixels + row_ref[...] * GRID_W + col_ref[...]).astype(F32)
    order = order_ref[...].astype(F32)
    slot = lax.broadcasted_iota(jnp.int32, (slots_here, 1), 0)
    slot = ((slot // sub) * tracks + track_here) * sub + slot % sub
    lane = lax.broadcasted_iota(jnp.int32, (slots_here, total), 1)
    picked = jnp.sum(jnp.where(lane == slot, order, 0.0), axis=1, keepdims=True)
    picked = picked.astype(jnp.int32)
    place = jnp.sum(jnp.where(lane == picked, code, 0.0), axis=1, keepdims=True)
    place = place.astype(jnp.int32) - me * pixels

    step = 512
    owned = jnp.zeros((slots_here, chan), F32)
    lane = lax.broadcasted_iota(jnp.int32, (slots_here, step), 1)
    for start in range(0, pixels, step):
        if start % piece == 0:
            maps_loads[start // piece].wait()
        hot = jnp.where(lane == place - start, 1.0, 0.0).astype(BF16)
        owned = owned + jnp.dot(hot, maps_ref[start : start + step, :], preferred_element_type=F32)
    owned = owned.astype(wire).reshape(frames, sub, chan)
    qpart[0:frames] = owned
    qpart[frames : 2 * frames] = owned

    pl.semaphore_wait(barrier, frames - 1)
    sends = []
    for st in range(stages):
        for off in range(1, frames):
            dest = lax.rem(me + off, frames)
            copy = pltpu.make_async_remote_copy(
                src_ref=qpart.at[pl.ds(lax.rem(dest + 1 + group * st, frames), group)],
                dst_ref=qrecv.at[off - 1, st],
                send_sem=qsend_sem.at[off - 1, st],
                recv_sem=qrecv_sem.at[off - 1, st],
                device_id={"frame": dest},
                device_id_type=MESH,
            )
            copy.start()
            sends.append(copy)

    k = lax.broadcasted_iota(jnp.int32, (2 * LANES, LANES), 0)
    n = lax.broadcasted_iota(jnp.int32, (2 * LANES, LANES), 1)
    down = k // GRID_W - n // GRID_W
    along = k % GRID_W - n % GRID_W + 1
    inside = (down >= 0) & (down < 3) & (along >= 0) & (along < 3)
    tap = jnp.where(inside, 3 * down + along, -1)
    for i in (5, 6, 7):
        loads[i].wait()
    span = 2 * LANES
    for h in range(hid):
        band = jnp.zeros((span, LANES), F32)
        for j in range(9):
            band = jnp.where(tap == j, weight_ref[h : h + 1, j : j + 1], band)
        high = band.astype(BF16)
        at = slice((h % 2) * LANES, (h % 2 + 1) * LANES)
        bands[h // 2, 0:span, at] = high
        bands[h // 2, span : 2 * span, at] = high
        bands[h // 2, 2 * span : 3 * span, at] = (band - high.astype(F32)).astype(BF16)

    for base in (0, span):
        xs[0:rows, base : base + GRID_W] = jnp.zeros((rows, GRID_W), BF16)
        xs[(tiles - 1) * rows : tiles * rows, base + LANES + GRID_W : base + span] = jnp.zeros(
            (rows, GRID_W), BF16
        )
    heads = [head_ref[0:1, h : h + 1] for h in range(hid)]
    floors = [-bias_ref[0:1, h : h + 1] for h in range(hid)]

    lane = lax.broadcasted_iota(jnp.int32, (rows, LANES), 1)
    low = (lane // GRID_W).astype(F32)
    colpos = (lane % GRID_W).astype(F32)
    scale = 1.0 / math.sqrt(chan)

    for st in range(stages):
        q = qpart[pl.ds(lax.rem(me + 1 + group * st, frames), group)].astype(F32)
        for off in range(1, frames):
            sends[st * (frames - 1) + off - 1].wait_recv()
            q = q + qrecv[off - 1, st].astype(F32)
        q = (q.reshape(rows, chan) * scale).astype(BF16)

        for i in range(0, tiles + 1, 2):
            first = max(LANES * i - GRID_W, 0)
            last = min(LANES * (i + 2) - GRID_W, pixels)
            cost = lax.dot_general(
                q, maps_ref[first:last, :], (((1,), (1,)), ((), ())), preferred_element_type=F32
            )
            high = cost.astype(BF16)
            rest = (cost - high.astype(F32)).astype(BF16)
            for base, value in ((0, high), (span, rest)):
                if i == 0:
                    xs[0:rows, base + GRID_W : base + LANES] = value[:, :GRID_W]
                    second = value[:, GRID_W : GRID_W + LANES]
                elif i == tiles:
                    xs[(i - 1) * rows : i * rows, base + LANES : base + LANES + GRID_W] = value
                    continue
                else:
                    xs[i * rows : (i + 1) * rows, base : base + LANES] = value[:, :LANES]
                    xs[(i - 1) * rows : i * rows, base + LANES : base + span] = value[:, :LANES]
                    second = value[:, LANES:]
                xs[i * rows : (i + 1) * rows, base + LANES : base + span] = second
                xs[(i + 1) * rows : (i + 2) * rows, base : base + LANES] = second

        chunk = min(256, tiles * rows)
        for start in range(0, tiles * rows, chunk):
            here = slice(start, start + chunk)
            left = jnp.concatenate([xs[here, :], xs[here, 0:span]], axis=1)
            total_here = jnp.zeros((chunk, LANES), F32)
            for h in range(0, hid, 2):
                y = jnp.dot(left, bands[h // 2], preferred_element_type=F32)
                total_here = total_here + heads[h] * jnp.maximum(y[:, :LANES], floors[h])
                total_here = total_here + heads[h + 1] * jnp.maximum(y[:, LANES:], floors[h + 1])
            logit[here, :] = total_here

        top = logit[0:rows, :]
        for i in range(1, tiles):
            top = jnp.maximum(top, logit[i * rows : (i + 1) * rows, :])
        top = jnp.max(top, axis=1, keepdims=True)
        mass = jnp.zeros((rows, LANES), F32)
        height = jnp.zeros((rows, LANES), F32)
        for i in range(tiles):
            e = jnp.exp(logit[i * rows : (i + 1) * rows, :] - top)
            logit[i * rows : (i + 1) * rows, :] = e
            mass = mass + e
            height = height + (2.0 * i) * e
        inv = 1.0 / jnp.sum(mass, axis=1, keepdims=True)
        row_est = jnp.sum(height + low * mass, axis=1, keepdims=True) * inv * (1.0 / (GRID_H - 1))
        col_est = jnp.sum(colpos * mass, axis=1, keepdims=True) * inv * (1.0 / (GRID_W - 1))
        sampled = jnp.zeros((rows, chan), F32)
        for i in range(0, tiles, 2):
            heat = jnp.concatenate(
                [
                    logit[i * rows : (i + 1) * rows, :] * inv,
                    logit[(i + 1) * rows : (i + 2) * rows, :] * inv,
                ],
                axis=1,
            ).astype(BF16)
            sampled = sampled + jnp.dot(
                heat, maps_ref[i * LANES : (i + 2) * LANES, :], preferred_element_type=F32
            )
        extra = jnp.where(lane == 0, row_est, jnp.where(lane == 1, col_est, 0.0))
        message = jnp.concatenate([sampled, extra], axis=1).astype(BF16).astype(wire)
        message = message.reshape(group, sub, chan + LANES)
        for g in range(group):
            j = st * group + g
            if j == frames - 1:
                srecv[me] = message[g]
            else:
                ssend[j] = message[g]
                copy = pltpu.make_async_remote_copy(
                    src_ref=ssend.at[j],
                    dst_ref=srecv.at[me],
                    send_sem=ssend_sem.at[j],
                    recv_sem=srecv_sem.at[j],
                    device_id={"frame": lax.rem(me + 1 + j, frames)},
                    device_id_type=MESH,
                )
                copy.start()
                sends.append(copy)

    for j in range(frames - 1):
        sends[stages * (frames - 1) + j].wait_recv()

    for i in (8, 9, 10, 11):
        loads[i].wait()
    got = srecv[...].astype(BF16) if wire != BF16 else srecv[...]
    rowcol = got[:, :, chan : chan + LANES].astype(F32)
    z = jnp.dot(
        got[:, :, :chan].reshape(slots_here, chan), mix_in_ref[...], preferred_element_type=F32
    )
    hidden = []
    for t in range(frames):
        mixed = taps_ref[1:2, :] * z[t * sub : (t + 1) * sub]
        if t > 0:
            mixed = taps_ref[0:1, :] * z[(t - 1) * sub : t * sub] + mixed
        if t < frames - 1:
            mixed = mixed + taps_ref[2:3, :] * z[(t + 1) * sub : (t + 2) * sub]
        mean = jnp.mean(mixed * mixed, axis=1, keepdims=True)
        normed = mixed * lax.rsqrt(mean + 1e-06) * gain_ref[...]
        hidden.append(jax.nn.gelu(normed).astype(BF16))
    delta = lax.dot_general(
        mix_out_ref[...],
        jnp.concatenate(hidden, axis=0),
        (((1,), (1,)), ((), ())),
        preferred_element_type=F32,
    )
    estimate = delta + rowcol.reshape(slots_here, LANES).T[0:3, :]
    for t in range(frames):
        for c in range(3):
            out_ref[c, t : t + 1, :] = estimate[c : c + 1, t * sub : (t + 1) * sub]

    for copy in sends:
        copy.wait_send()


def on_device(
    feature_maps,
    query_frame,
    query_row,
    query_col,
    track_order,
    conv_weight,
    conv_bias,
    head_weight,
    mix_in,
    temporal_taps,
    mix_gain,
    mix_out,
):
    frames = lax.axis_size("frame")
    tracks = lax.axis_size("track")
    _, pixels, chan = feature_maps.shape
    total = track_order.shape[0]
    sub = total // (tracks * frames)
    hid = conv_weight.shape[0]
    mixw = mix_in.shape[1]
    wire = BF16 if sub % 16 == 0 else F32
    group = max(1, min(frames, 64 // sub))
    while frames % group:
        group -= 1
    stages = frames // group
    rows = group * sub
    tiles = pixels // LANES
    dma = pltpu.SemaphoreType.DMA
    args = (
        feature_maps.reshape(pixels, chan),
        query_frame.reshape(1, total),
        query_row.reshape(1, total),
        query_col.reshape(1, total),
        track_order.reshape(1, total),
        conv_weight,
        conv_bias.reshape(1, hid),
        head_weight.reshape(1, hid),
        mix_in,
        temporal_taps,
        mix_gain.reshape(1, mixw),
        mix_out.T,
    )
    out = pl.pallas_call(
        functools.partial(kernel, (frames, tracks, sub, group, wire)),
        out_shape=jax.ShapeDtypeStruct((3, frames, sub), F32),
        in_specs=[pl.BlockSpec(memory_space=pl.ANY)] * len(args),
        out_specs=pl.BlockSpec(memory_space=pltpu.VMEM),
        scratch_shapes=[pltpu.VMEM(x.shape, x.dtype) for x in args]
        + [
            pltpu.VMEM((2 * frames, sub, chan), wire),
            pltpu.VMEM((frames - 1, stages, group, sub, chan), wire),
            pltpu.VMEM((tiles * rows, 4 * LANES), BF16),
            pltpu.VMEM((hid // 2, 6 * LANES, 2 * LANES), BF16),
            pltpu.VMEM((tiles * rows, LANES), F32),
            pltpu.VMEM((frames - 1, sub, chan + LANES), wire),
            pltpu.VMEM((frames, sub, chan + LANES), wire),
            dma((frames - 1, stages)),
            dma((frames - 1, stages)),
            dma((frames - 1,)),
            dma((frames - 1,)),
            dma((len(args),)),
            dma((4,)),
        ],
        compiler_params=pltpu.CompilerParams(
            collective_id=0, has_side_effects=True, vmem_limit_bytes=62 * 1024 * 1024
        ),
    )(*args)
    return out.transpose(2, 0, 1)


def solution(mesh):
    placed = (
        P(("clip", "frame"), None, None),
        P("clip"),
        P("clip"),
        P("clip"),
        P("clip"),
        P(),
        P(),
        P(),
        P(),
        P(),
        P(),
        P(),
    )
    return jax.shard_map(
        on_device,
        mesh=mesh,
        in_specs=placed,
        out_specs=P(("clip", "frame", "track"), None, None),
        check_vma=False,
    )
```

```python
import functools
import math

import jax
import jax.numpy as jnp
from jax import lax
from jax.experimental import pallas as pl
from jax.experimental.pallas import tpu as pltpu
from jax.sharding import PartitionSpec as P

GRID_H = 64
GRID_W = 64
MESH = pl.DeviceIdType.MESH
LANES = 128
F32 = jnp.float32
BF16 = jnp.bfloat16
F8 = jnp.float8_e5m2


def kernel(
    dims,
    *refs,
):
    count = 12
    sources = refs[:count]
    out_ref = refs[count]
    held = refs[count + 1 : 2 * count + 1]
    (
        maps_ref,
        frame_ref,
        row_ref,
        col_ref,
        order_ref,
        weight_ref,
        bias_ref,
        head_ref,
        mix_in_ref,
        taps_ref,
        gain_ref,
        mix_out_ref,
    ) = held
    (
        qpart,
        qrecv,
        xs,
        xs8,
        bands,
        bands8,
        logit,
        ssend,
        srecv,
        qsend_sem,
        qrecv_sem,
        ssend_sem,
        srecv_sem,
        load_sem,
        maps_sem,
    ) = refs[2 * count + 1 :]
    frames, tracks, sub, group, wire = dims
    stages = frames // group
    rows = group * sub
    pixels, chan = maps_ref.shape
    total = order_ref.shape[1]
    slots_here = frames * sub
    hid = weight_ref.shape[0]
    tiles = pixels // LANES
    me = lax.axis_index("frame")
    track_here = lax.axis_index("track")

    barrier = pltpu.get_barrier_semaphore()
    for off in range(1, frames):
        pl.semaphore_signal(
            barrier, inc=1, device_id={"frame": lax.rem(me + off, frames)}, device_id_type=MESH
        )

    pieces = maps_sem.shape[0]
    piece = pixels // pieces
    loads = {}
    for i in (1, 2, 3, 4):
        loads[i] = pltpu.make_async_copy(sources[i], held[i], load_sem.at[i])
        loads[i].start()
    maps_loads = []
    for i in range(pieces):
        part = pl.ds(i * piece, piece)
        copy = pltpu.make_async_copy(sources[0].at[part], maps_ref.at[part], maps_sem.at[i])
        copy.start()
        maps_loads.append(copy)
    for i in (5, 6, 7, 8, 9, 10, 11):
        loads[i] = pltpu.make_async_copy(sources[i], held[i], load_sem.at[i])
        loads[i].start()
    for i in (1, 2, 3, 4):
        loads[i].wait()

    code = (frame_ref[...] * pixels + row_ref[...] * GRID_W + col_ref[...]).astype(F32)
    order = order_ref[...].astype(F32)
    slot = lax.broadcasted_iota(jnp.int32, (slots_here, 1), 0)
    slot = ((slot // sub) * tracks + track_here) * sub + slot % sub
    lane = lax.broadcasted_iota(jnp.int32, (slots_here, total), 1)
    picked = jnp.sum(jnp.where(lane == slot, order, 0.0), axis=1, keepdims=True)
    picked = picked.astype(jnp.int32)
    place = jnp.sum(jnp.where(lane == picked, code, 0.0), axis=1, keepdims=True)
    place = place.astype(jnp.int32) - me * pixels

    step = 512
    owned = jnp.zeros((slots_here, chan), F32)
    lane = lax.broadcasted_iota(jnp.int32, (slots_here, step), 1)
    for start in range(0, pixels, step):
        if start % piece == 0:
            maps_loads[start // piece].wait()
        hot = jnp.where(lane == place - start, 1.0, 0.0).astype(BF16)
        owned = owned + jnp.dot(hot, maps_ref[start : start + step, :], preferred_element_type=F32)
    owned = owned.astype(wire).reshape(frames, sub, chan)
    qpart[0:frames] = owned
    qpart[frames : 2 * frames] = owned

    pl.semaphore_wait(barrier, frames - 1)
    sends = []
    for st in range(stages):
        for off in range(1, frames):
            dest = lax.rem(me + off, frames)
            copy = pltpu.make_async_remote_copy(
                src_ref=qpart.at[pl.ds(lax.rem(dest + 1 + group * st, frames), group)],
                dst_ref=qrecv.at[off - 1, st],
                send_sem=qsend_sem.at[off - 1, st],
                recv_sem=qrecv_sem.at[off - 1, st],
                device_id={"frame": dest},
                device_id_type=MESH,
            )
            copy.start()
            sends.append(copy)

    k = lax.broadcasted_iota(jnp.int32, (2 * LANES, LANES), 0)
    n = lax.broadcasted_iota(jnp.int32, (2 * LANES, LANES), 1)
    down = k // GRID_W - n // GRID_W
    along = k % GRID_W - n % GRID_W + 1
    inside = (down >= 0) & (down < 3) & (along >= 0) & (along < 3)
    tap = jnp.where(inside, 3 * down + along, -1)
    for i in (5, 6, 7):
        loads[i].wait()
    span = 2 * LANES
    for h in range(hid):
        band = jnp.zeros((span, LANES), F32)
        for j in range(9):
            band = jnp.where(tap == j, weight_ref[h : h + 1, j : j + 1], band)
        high = band.astype(BF16)
        at = slice((h % 2) * LANES, (h % 2 + 1) * LANES)
        bands[h // 2, :, at] = high
        bands8[h // 2, 0:span, at] = band.astype(F8)
        bands8[h // 2, span : 2 * span, at] = (band - high.astype(F32)).astype(F8)

    for held_in, base in ((xs, 0), (xs8, 0), (xs8, span)):
        blank = jnp.zeros((rows, GRID_W), held_in.dtype)
        held_in[0:rows, base : base + GRID_W] = blank
        held_in[(tiles - 1) * rows : tiles * rows, base + LANES + GRID_W : base + span] = blank
    heads = [head_ref[0:1, h : h + 1] for h in range(hid)]
    floors = [-bias_ref[0:1, h : h + 1] for h in range(hid)]

    lane = lax.broadcasted_iota(jnp.int32, (rows, LANES), 1)
    low = (lane // GRID_W).astype(F32)
    colpos = (lane % GRID_W).astype(F32)
    scale = 1.0 / math.sqrt(chan)

    for st in range(stages):
        q = qpart[pl.ds(lax.rem(me + 1 + group * st, frames), group)].astype(F32)
        for off in range(1, frames):
            sends[st * (frames - 1) + off - 1].wait_recv()
            q = q + qrecv[off - 1, st].astype(F32)
        q = (q.reshape(rows, chan) * scale).astype(BF16)

        for i in range(0, tiles + 1, 2):
            first = max(LANES * i - GRID_W, 0)
            last = min(LANES * (i + 2) - GRID_W, pixels)
            cost = lax.dot_general(
                q, maps_ref[first:last, :], (((1,), (1,)), ((), ())), preferred_element_type=F32
            )
            high = cost.astype(BF16)
            rest = (cost - high.astype(F32)).astype(F8)
            for out, base, value in ((xs, 0, high), (xs8, 0, rest), (xs8, span, cost.astype(F8))):
                if i == 0:
                    out[0:rows, base + GRID_W : base + LANES] = value[:, :GRID_W]
                    second = value[:, GRID_W : GRID_W + LANES]
                elif i == tiles:
                    out[(i - 1) * rows : i * rows, base + LANES : base + LANES + GRID_W] = value
                    continue
                else:
                    out[i * rows : (i + 1) * rows, base : base + LANES] = value[:, :LANES]
                    out[(i - 1) * rows : i * rows, base + LANES : base + span] = value[:, :LANES]
                    second = value[:, LANES:]
                out[i * rows : (i + 1) * rows, base + LANES : base + span] = second
                out[(i + 1) * rows : (i + 2) * rows, base : base + LANES] = second

        chunk = min(256, tiles * rows)
        for start in range(0, tiles * rows, chunk):
            here = slice(start, start + chunk)
            left = xs[here, :]
            left8 = xs8[here, :]
            total_here = jnp.zeros((chunk, LANES), F32)
            for h in range(0, hid, 2):
                y = jnp.dot(left, bands[h // 2], preferred_element_type=F32)
                y = y + jnp.dot(left8, bands8[h // 2], preferred_element_type=F32)
                total_here = total_here + heads[h] * jnp.maximum(y[:, :LANES], floors[h])
                total_here = total_here + heads[h + 1] * jnp.maximum(y[:, LANES:], floors[h + 1])
            logit[here, :] = total_here

        top = logit[0:rows, :]
        for i in range(1, tiles):
            top = jnp.maximum(top, logit[i * rows : (i + 1) * rows, :])
        top = jnp.max(top, axis=1, keepdims=True)
        mass = jnp.zeros((rows, LANES), F32)
        height = jnp.zeros((rows, LANES), F32)
        for i in range(tiles):
            e = jnp.exp(logit[i * rows : (i + 1) * rows, :] - top)
            logit[i * rows : (i + 1) * rows, :] = e
            mass = mass + e
            height = height + (2.0 * i) * e
        inv = 1.0 / jnp.sum(mass, axis=1, keepdims=True)
        row_est = jnp.sum(height + low * mass, axis=1, keepdims=True) * inv * (1.0 / (GRID_H - 1))
        col_est = jnp.sum(colpos * mass, axis=1, keepdims=True) * inv * (1.0 / (GRID_W - 1))
        sampled = jnp.zeros((rows, chan), F32)
        for i in range(0, tiles, 2):
            heat = jnp.concatenate(
                [
                    logit[i * rows : (i + 1) * rows, :] * inv,
                    logit[(i + 1) * rows : (i + 2) * rows, :] * inv,
                ],
                axis=1,
            ).astype(BF16)
            sampled = sampled + jnp.dot(
                heat, maps_ref[i * LANES : (i + 2) * LANES, :], preferred_element_type=F32
            )
        extra = jnp.where(lane == 0, row_est, jnp.where(lane == 1, col_est, 0.0))
        message = jnp.concatenate([sampled, extra], axis=1).astype(BF16).astype(wire)
        message = message.reshape(group, sub, chan + LANES)
        for g in range(group):
            j = st * group + g
            if j == frames - 1:
                srecv[me] = message[g]
            else:
                ssend[j] = message[g]
                copy = pltpu.make_async_remote_copy(
                    src_ref=ssend.at[j],
                    dst_ref=srecv.at[me],
                    send_sem=ssend_sem.at[j],
                    recv_sem=srecv_sem.at[j],
                    device_id={"frame": lax.rem(me + 1 + j, frames)},
                    device_id_type=MESH,
                )
                copy.start()
                sends.append(copy)

    for j in range(frames - 1):
        sends[stages * (frames - 1) + j].wait_recv()

    for i in (8, 9, 10, 11):
        loads[i].wait()
    got = srecv[...].astype(BF16) if wire != BF16 else srecv[...]
    rowcol = got[:, :, chan : chan + LANES].astype(F32)
    z = jnp.dot(
        got[:, :, :chan].reshape(slots_here, chan), mix_in_ref[...], preferred_element_type=F32
    )
    hidden = []
    for t in range(frames):
        mixed = taps_ref[1:2, :] * z[t * sub : (t + 1) * sub]
        if t > 0:
            mixed = taps_ref[0:1, :] * z[(t - 1) * sub : t * sub] + mixed
        if t < frames - 1:
            mixed = mixed + taps_ref[2:3, :] * z[(t + 1) * sub : (t + 2) * sub]
        mean = jnp.mean(mixed * mixed, axis=1, keepdims=True)
        normed = mixed * lax.rsqrt(mean + 1e-06) * gain_ref[...]
        hidden.append(jax.nn.gelu(normed).astype(BF16))
    delta = lax.dot_general(
        mix_out_ref[...],
        jnp.concatenate(hidden, axis=0),
        (((1,), (1,)), ((), ())),
        preferred_element_type=F32,
    )
    estimate = delta + rowcol.reshape(slots_here, LANES).T[0:3, :]
    for t in range(frames):
        for c in range(3):
            out_ref[c, t : t + 1, :] = estimate[c : c + 1, t * sub : (t + 1) * sub]

    for copy in sends:
        copy.wait_send()


def on_device(
    feature_maps,
    query_frame,
    query_row,
    query_col,
    track_order,
    conv_weight,
    conv_bias,
    head_weight,
    mix_in,
    temporal_taps,
    mix_gain,
    mix_out,
):
    frames = lax.axis_size("frame")
    tracks = lax.axis_size("track")
    _, pixels, chan = feature_maps.shape
    total = track_order.shape[0]
    sub = total // (tracks * frames)
    hid = conv_weight.shape[0]
    mixw = mix_in.shape[1]
    wire = BF16 if sub % 16 == 0 else F32
    group = max(1, min(frames, 64 // sub))
    while frames % group:
        group -= 1
    stages = frames // group
    rows = group * sub
    tiles = pixels // LANES
    dma = pltpu.SemaphoreType.DMA
    args = (
        feature_maps.reshape(pixels, chan),
        query_frame.reshape(1, total),
        query_row.reshape(1, total),
        query_col.reshape(1, total),
        track_order.reshape(1, total),
        conv_weight,
        conv_bias.reshape(1, hid),
        head_weight.reshape(1, hid),
        mix_in,
        temporal_taps,
        mix_gain.reshape(1, mixw),
        mix_out.T,
    )
    out = pl.pallas_call(
        functools.partial(kernel, (frames, tracks, sub, group, wire)),
        out_shape=jax.ShapeDtypeStruct((3, frames, sub), F32),
        in_specs=[pl.BlockSpec(memory_space=pl.ANY)] * len(args),
        out_specs=pl.BlockSpec(memory_space=pltpu.VMEM),
        scratch_shapes=[pltpu.VMEM(x.shape, x.dtype) for x in args]
        + [
            pltpu.VMEM((2 * frames, sub, chan), wire),
            pltpu.VMEM((frames - 1, stages, group, sub, chan), wire),
            pltpu.VMEM((tiles * rows, 2 * LANES), BF16),
            pltpu.VMEM((tiles * rows, 4 * LANES), F8),
            pltpu.VMEM((hid // 2, 2 * LANES, 2 * LANES), BF16),
            pltpu.VMEM((hid // 2, 4 * LANES, 2 * LANES), F8),
            pltpu.VMEM((tiles * rows, LANES), F32),
            pltpu.VMEM((frames - 1, sub, chan + LANES), wire),
            pltpu.VMEM((frames, sub, chan + LANES), wire),
            dma((frames - 1, stages)),
            dma((frames - 1, stages)),
            dma((frames - 1,)),
            dma((frames - 1,)),
            dma((len(args),)),
            dma((4,)),
        ],
        compiler_params=pltpu.CompilerParams(
            collective_id=0, has_side_effects=True, vmem_limit_bytes=62 * 1024 * 1024
        ),
    )(*args)
    return out.transpose(2, 0, 1)


def solution(mesh):
    placed = (
        P(("clip", "frame"), None, None),
        P("clip"),
        P("clip"),
        P("clip"),
        P("clip"),
        P(),
        P(),
        P(),
        P(),
        P(),
        P(),
        P(),
    )
    return jax.shard_map(
        on_device,
        mesh=mesh,
        in_specs=placed,
        out_specs=P(("clip", "frame", "track"), None, None),
        check_vma=False,
    )
```

```python
import functools
import math

import jax
import jax.numpy as jnp
from jax import lax
from jax.experimental import pallas as pl
from jax.experimental.pallas import tpu as pltpu
from jax.sharding import PartitionSpec as P

GRID_H = 64
GRID_W = 64
MESH = pl.DeviceIdType.MESH
LANES = 128
F32 = jnp.float32
BF16 = jnp.bfloat16
F8 = jnp.float8_e5m2


def kernel(
    dims,
    *refs,
):
    count = 12
    sources = refs[:count]
    out_ref = refs[count]
    held = refs[count + 1 : 2 * count + 1]
    (
        maps_ref,
        frame_ref,
        row_ref,
        col_ref,
        order_ref,
        weight_ref,
        bias_ref,
        head_ref,
        mix_in_ref,
        taps_ref,
        gain_ref,
        mix_out_ref,
    ) = held
    (
        qpart,
        qrecv,
        xs,
        xs8,
        bands,
        bands8,
        logit,
        ssend,
        srecv,
        qsend_sem,
        qrecv_sem,
        ssend_sem,
        srecv_sem,
        load_sem,
        maps_sem,
    ) = refs[2 * count + 1 :]
    frames, tracks, sub, stages, wire = dims
    pixels, chan = maps_ref.shape
    total = order_ref.shape[1]
    slots_here = frames * sub
    hid = weight_ref.shape[0]
    tiles = pixels // LANES
    me = lax.axis_index("frame")
    track_here = lax.axis_index("track")

    barrier = pltpu.get_barrier_semaphore()
    for off in range(1, frames):
        pl.semaphore_signal(
            barrier, inc=1, device_id={"frame": lax.rem(me + off, frames)}, device_id_type=MESH
        )

    pieces = maps_sem.shape[0]
    piece = pixels // pieces
    loads = {}
    for i in (1, 2, 3, 4):
        loads[i] = pltpu.make_async_copy(sources[i], held[i], load_sem.at[i])
        loads[i].start()
    maps_loads = []
    for i in range(pieces):
        part = pl.ds(i * piece, piece)
        copy = pltpu.make_async_copy(sources[0].at[part], maps_ref.at[part], maps_sem.at[i])
        copy.start()
        maps_loads.append(copy)
    for i in (5, 6, 7, 8, 9, 10, 11):
        loads[i] = pltpu.make_async_copy(sources[i], held[i], load_sem.at[i])
        loads[i].start()
    for i in (1, 2, 3, 4):
        loads[i].wait()

    code = (frame_ref[...] * pixels + row_ref[...] * GRID_W + col_ref[...]).astype(F32)
    order = order_ref[...].astype(F32)
    slot = lax.broadcasted_iota(jnp.int32, (slots_here, 1), 0)
    slot = ((slot // sub) * tracks + track_here) * sub + slot % sub
    lane = lax.broadcasted_iota(jnp.int32, (slots_here, total), 1)
    picked = jnp.sum(jnp.where(lane == slot, order, 0.0), axis=1, keepdims=True)
    picked = picked.astype(jnp.int32)
    place = jnp.sum(jnp.where(lane == picked, code, 0.0), axis=1, keepdims=True)
    place = place.astype(jnp.int32) - me * pixels

    step = 512
    owned = jnp.zeros((slots_here, chan), F32)
    lane = lax.broadcasted_iota(jnp.int32, (slots_here, step), 1)
    for start in range(0, pixels, step):
        if start % piece == 0:
            maps_loads[start // piece].wait()
        hot = jnp.where(lane == place - start, 1.0, 0.0).astype(BF16)
        owned = owned + jnp.dot(hot, maps_ref[start : start + step, :], preferred_element_type=F32)
    owned = owned.astype(wire).reshape(frames, sub, chan)
    qpart[0:frames] = owned
    qpart[frames : 2 * frames] = owned

    pl.semaphore_wait(barrier, frames - 1)
    queries = []
    for st, (begin, group) in enumerate(stages):
        copies = []
        for off in range(1, frames):
            dest = lax.rem(me + off, frames)
            copies.append(
                pltpu.make_async_remote_copy(
                    src_ref=qpart.at[pl.ds(lax.rem(dest + 1 + begin, frames), group)],
                    dst_ref=qrecv.at[off - 1, pl.ds(begin, group)],
                    send_sem=qsend_sem.at[off - 1, st],
                    recv_sem=qrecv_sem.at[off - 1, st],
                    device_id={"frame": dest},
                    device_id_type=MESH,
                )
            )
        queries.append(copies)
    for copy in queries[0]:
        copy.start()

    k = lax.broadcasted_iota(jnp.int32, (2 * LANES, LANES), 0)
    n = lax.broadcasted_iota(jnp.int32, (2 * LANES, LANES), 1)
    down = k // GRID_W - n // GRID_W
    along = k % GRID_W - n % GRID_W + 1
    inside = (down >= 0) & (down < 3) & (along >= 0) & (along < 3)
    tap = jnp.where(inside, 3 * down + along, -1)
    for i in (5, 6, 7):
        loads[i].wait()
    span = 2 * LANES
    for h in range(hid):
        band = jnp.zeros((span, LANES), F32)
        for j in range(9):
            band = jnp.where(tap == j, weight_ref[h : h + 1, j : j + 1], band)
        high = band.astype(BF16)
        at = slice((h % 2) * LANES, (h % 2 + 1) * LANES)
        bands[h // 2, :, at] = high
        bands8[h // 2, 0:span, at] = band.astype(F8)
        bands8[h // 2, span : 2 * span, at] = (band - high.astype(F32)).astype(F8)

    heads = [head_ref[0:1, h : h + 1] for h in range(hid)]
    floors = [-bias_ref[0:1, h : h + 1] for h in range(hid)]

    scale = 1.0 / math.sqrt(chan)

    for copies in queries[1:2]:
        for copy in copies:
            copy.start()
    sends = []

    for st, (begin, group) in enumerate(stages):
        rows = group * sub
        lane = lax.broadcasted_iota(jnp.int32, (rows, LANES), 1)
        low = (lane // GRID_W).astype(F32)
        colpos = (lane % GRID_W).astype(F32)
        for held_in, base in ((xs, 0), (xs8, 0), (xs8, span)):
            blank = jnp.zeros((rows, GRID_W), held_in.dtype)
            held_in[0:rows, base : base + GRID_W] = blank
            held_in[(tiles - 1) * rows : tiles * rows, base + LANES + GRID_W : base + span] = blank
        q = qpart[pl.ds(lax.rem(me + 1 + begin, frames), group)].astype(F32)
        for off in range(1, frames):
            queries[st][off - 1].wait_recv()
            q = q + qrecv[off - 1, begin : begin + group].astype(F32)
        q = (q.reshape(rows, chan) * scale).astype(BF16)
        for copies in queries[st + 2 : st + 3]:
            for copy in copies:
                copy.start()

        for i in range(0, tiles + 1, 2):
            first = max(LANES * i - GRID_W, 0)
            last = min(LANES * (i + 2) - GRID_W, pixels)
            cost = lax.dot_general(
                q, maps_ref[first:last, :], (((1,), (1,)), ((), ())), preferred_element_type=F32
            )
            high = cost.astype(BF16)
            rest = (cost - high.astype(F32)).astype(F8)
            for out, base, value in ((xs, 0, high), (xs8, 0, rest), (xs8, span, cost.astype(F8))):
                if i == 0:
                    out[0:rows, base + GRID_W : base + LANES] = value[:, :GRID_W]
                    second = value[:, GRID_W : GRID_W + LANES]
                elif i == tiles:
                    out[(i - 1) * rows : i * rows, base + LANES : base + LANES + GRID_W] = value
                    continue
                else:
                    out[i * rows : (i + 1) * rows, base : base + LANES] = value[:, :LANES]
                    out[(i - 1) * rows : i * rows, base + LANES : base + span] = value[:, :LANES]
                    second = value[:, LANES:]
                out[i * rows : (i + 1) * rows, base + LANES : base + span] = second
                out[(i + 1) * rows : (i + 2) * rows, base : base + LANES] = second

        chunk = min(256, tiles * rows)
        for start in range(0, tiles * rows, chunk):
            here = slice(start, start + chunk)
            left = xs[here, :]
            left8 = xs8[here, :]
            total_here = jnp.zeros((chunk, LANES), F32)
            for h in range(0, hid, 2):
                y = jnp.dot(left, bands[h // 2], preferred_element_type=F32)
                y = y + jnp.dot(left8, bands8[h // 2], preferred_element_type=F32)
                total_here = total_here + heads[h] * jnp.maximum(y[:, :LANES], floors[h])
                total_here = total_here + heads[h + 1] * jnp.maximum(y[:, LANES:], floors[h + 1])
            logit[here, :] = total_here

        top = logit[0:rows, :]
        for i in range(1, tiles):
            top = jnp.maximum(top, logit[i * rows : (i + 1) * rows, :])
        top = jnp.max(top, axis=1, keepdims=True)
        mass = jnp.zeros((rows, LANES), F32)
        height = jnp.zeros((rows, LANES), F32)
        for i in range(tiles):
            e = jnp.exp(logit[i * rows : (i + 1) * rows, :] - top)
            logit[i * rows : (i + 1) * rows, :] = e
            mass = mass + e
            height = height + (2.0 * i) * e
        inv = 1.0 / jnp.sum(mass, axis=1, keepdims=True)
        row_est = jnp.sum(height + low * mass, axis=1, keepdims=True) * inv * (1.0 / (GRID_H - 1))
        col_est = jnp.sum(colpos * mass, axis=1, keepdims=True) * inv * (1.0 / (GRID_W - 1))
        sampled = jnp.zeros((rows, chan), F32)
        for i in range(0, tiles, 2):
            heat = jnp.concatenate(
                [
                    logit[i * rows : (i + 1) * rows, :] * inv,
                    logit[(i + 1) * rows : (i + 2) * rows, :] * inv,
                ],
                axis=1,
            ).astype(BF16)
            sampled = sampled + jnp.dot(
                heat, maps_ref[i * LANES : (i + 2) * LANES, :], preferred_element_type=F32
            )
        extra = jnp.where(lane == 0, row_est, jnp.where(lane == 1, col_est, 0.0))
        message = jnp.concatenate([sampled, extra], axis=1).astype(BF16).astype(wire)
        message = message.reshape(group, sub, chan + LANES)
        for g in range(group):
            j = begin + g
            if j == frames - 1:
                srecv[me] = message[g]
            else:
                ssend[j] = message[g]
                copy = pltpu.make_async_remote_copy(
                    src_ref=ssend.at[j],
                    dst_ref=srecv.at[me],
                    send_sem=ssend_sem.at[j],
                    recv_sem=srecv_sem.at[j],
                    device_id={"frame": lax.rem(me + 1 + j, frames)},
                    device_id_type=MESH,
                )
                copy.start()
                sends.append(copy)

    for j in range(frames - 1):
        sends[j].wait_recv()

    for i in (8, 9, 10, 11):
        loads[i].wait()
    got = srecv[...].astype(BF16) if wire != BF16 else srecv[...]
    rowcol = got[:, :, chan : chan + LANES].astype(F32)
    z = jnp.dot(
        got[:, :, :chan].reshape(slots_here, chan), mix_in_ref[...], preferred_element_type=F32
    )
    hidden = []
    for t in range(frames):
        mixed = taps_ref[1:2, :] * z[t * sub : (t + 1) * sub]
        if t > 0:
            mixed = taps_ref[0:1, :] * z[(t - 1) * sub : t * sub] + mixed
        if t < frames - 1:
            mixed = mixed + taps_ref[2:3, :] * z[(t + 1) * sub : (t + 2) * sub]
        mean = jnp.mean(mixed * mixed, axis=1, keepdims=True)
        normed = mixed * lax.rsqrt(mean + 1e-06) * gain_ref[...]
        hidden.append(jax.nn.gelu(normed).astype(BF16))
    delta = lax.dot_general(
        mix_out_ref[...],
        jnp.concatenate(hidden, axis=0),
        (((1,), (1,)), ((), ())),
        preferred_element_type=F32,
    )
    estimate = delta + rowcol.reshape(slots_here, LANES).T[0:3, :]
    for t in range(frames):
        for c in range(3):
            out_ref[c, t : t + 1, :] = estimate[c : c + 1, t * sub : (t + 1) * sub]

    for copy in [copy for copies in queries for copy in copies] + sends:
        copy.wait_send()


def on_device(
    feature_maps,
    query_frame,
    query_row,
    query_col,
    track_order,
    conv_weight,
    conv_bias,
    head_weight,
    mix_in,
    temporal_taps,
    mix_gain,
    mix_out,
):
    frames = lax.axis_size("frame")
    tracks = lax.axis_size("track")
    _, pixels, chan = feature_maps.shape
    total = track_order.shape[0]
    sub = total // (tracks * frames)
    hid = conv_weight.shape[0]
    mixw = mix_in.shape[1]
    wire = BF16 if sub % 16 == 0 else F32
    unit = max(1, min(frames, 32 // sub))
    cuts = sorted({0, unit, max(unit, frames - unit), frames})
    stages = [(begin, end - begin) for begin, end in zip(cuts, cuts[1:])]
    rows = sub * max(group for _, group in stages)
    tiles = pixels // LANES
    dma = pltpu.SemaphoreType.DMA
    args = (
        feature_maps.reshape(pixels, chan),
        query_frame.reshape(1, total),
        query_row.reshape(1, total),
        query_col.reshape(1, total),
        track_order.reshape(1, total),
        conv_weight,
        conv_bias.reshape(1, hid),
        head_weight.reshape(1, hid),
        mix_in,
        temporal_taps,
        mix_gain.reshape(1, mixw),
        mix_out.T,
    )
    out = pl.pallas_call(
        functools.partial(kernel, (frames, tracks, sub, stages, wire)),
        out_shape=jax.ShapeDtypeStruct((3, frames, sub), F32),
        in_specs=[pl.BlockSpec(memory_space=pl.ANY)] * len(args),
        out_specs=pl.BlockSpec(memory_space=pltpu.VMEM),
        scratch_shapes=[pltpu.VMEM(x.shape, x.dtype) for x in args]
        + [
            pltpu.VMEM((2 * frames, sub, chan), wire),
            pltpu.VMEM((frames - 1, frames, sub, chan), wire),
            pltpu.VMEM((tiles * rows, 2 * LANES), BF16),
            pltpu.VMEM((tiles * rows, 4 * LANES), F8),
            pltpu.VMEM((hid // 2, 2 * LANES, 2 * LANES), BF16),
            pltpu.VMEM((hid // 2, 4 * LANES, 2 * LANES), F8),
            pltpu.VMEM((tiles * rows, LANES), F32),
            pltpu.VMEM((frames - 1, sub, chan + LANES), wire),
            pltpu.VMEM((frames, sub, chan + LANES), wire),
            dma((frames - 1, len(stages))),
            dma((frames - 1, len(stages))),
            dma((frames - 1,)),
            dma((frames - 1,)),
            dma((len(args),)),
            dma((4,)),
        ],
        compiler_params=pltpu.CompilerParams(
            collective_id=0, has_side_effects=True, vmem_limit_bytes=56 * 1024 * 1024
        ),
    )(*args)
    return out.transpose(2, 0, 1)


def solution(mesh):
    placed = (
        P(("clip", "frame"), None, None),
        P("clip"),
        P("clip"),
        P("clip"),
        P("clip"),
        P(),
        P(),
        P(),
        P(),
        P(),
        P(),
        P(),
    )
    return jax.shard_map(
        on_device,
        mesh=mesh,
        in_specs=placed,
        out_specs=P(("clip", "frame", "track"), None, None),
        check_vma=False,
    )
```

```python
import functools
import math

import jax
import jax.numpy as jnp
from jax import lax
from jax.experimental import pallas as pl
from jax.experimental.pallas import tpu as pltpu
from jax.sharding import PartitionSpec as P

GRID_H = 64
GRID_W = 64
MESH = pl.DeviceIdType.MESH
LANES = 128
F32 = jnp.float32
BF16 = jnp.bfloat16
F8 = jnp.float8_e5m2


def kernel(
    dims,
    *refs,
):
    count = 12
    sources = refs[:count]
    out_ref = refs[count]
    held = refs[count + 1 : 2 * count + 1]
    (
        maps_ref,
        frame_ref,
        row_ref,
        col_ref,
        order_ref,
        weight_ref,
        bias_ref,
        head_ref,
        mix_in_ref,
        taps_ref,
        gain_ref,
        mix_out_ref,
    ) = held
    (
        qpart,
        qrecv,
        xs_all,
        xs8_all,
        bands,
        bands8,
        logit_all,
        ssend,
        srecv,
        qsend_sem,
        qrecv_sem,
        ssend_sem,
        srecv_sem,
        load_sem,
        maps_sem,
    ) = refs[2 * count + 1 :]
    frames, tracks, sub, stages, wire = dims
    pixels, chan = maps_ref.shape
    total = order_ref.shape[1]
    slots_here = frames * sub
    hid = weight_ref.shape[0]
    tiles = pixels // LANES
    me = lax.axis_index("frame")
    track_here = lax.axis_index("track")

    barrier = pltpu.get_barrier_semaphore()
    for off in range(1, frames):
        pl.semaphore_signal(
            barrier, inc=1, device_id={"frame": lax.rem(me + off, frames)}, device_id_type=MESH
        )

    pieces = maps_sem.shape[0]
    piece = pixels // pieces
    loads = {}
    for i in (1, 2, 3, 4):
        loads[i] = pltpu.make_async_copy(sources[i], held[i], load_sem.at[i])
        loads[i].start()
    maps_loads = []
    for i in range(pieces):
        part = pl.ds(i * piece, piece)
        copy = pltpu.make_async_copy(sources[0].at[part], maps_ref.at[part], maps_sem.at[i])
        copy.start()
        maps_loads.append(copy)
    for i in (5, 6, 7, 8, 9, 10, 11):
        loads[i] = pltpu.make_async_copy(sources[i], held[i], load_sem.at[i])
        loads[i].start()
    for i in (1, 2, 3, 4):
        loads[i].wait()

    code = (frame_ref[...] * pixels + row_ref[...] * GRID_W + col_ref[...]).astype(F32)
    order = order_ref[...].astype(F32)
    slot = lax.broadcasted_iota(jnp.int32, (slots_here, 1), 0)
    slot = ((slot // sub) * tracks + track_here) * sub + slot % sub
    lane = lax.broadcasted_iota(jnp.int32, (slots_here, total), 1)
    picked = jnp.sum(jnp.where(lane == slot, order, 0.0), axis=1, keepdims=True)
    picked = picked.astype(jnp.int32)
    place = jnp.sum(jnp.where(lane == picked, code, 0.0), axis=1, keepdims=True)
    place = place.astype(jnp.int32) - me * pixels

    step = 512
    owned = jnp.zeros((slots_here, chan), F32)
    lane = lax.broadcasted_iota(jnp.int32, (slots_here, step), 1)
    for start in range(0, pixels, step):
        if start % piece == 0:
            maps_loads[start // piece].wait()
        hot = jnp.where(lane == place - start, 1.0, 0.0).astype(BF16)
        owned = owned + jnp.dot(hot, maps_ref[start : start + step, :], preferred_element_type=F32)
    owned = owned.astype(wire).reshape(frames, sub, chan)
    qpart[0:frames] = owned
    qpart[frames : 2 * frames] = owned

    pl.semaphore_wait(barrier, frames - 1)
    queries = []
    for st, (begin, group) in enumerate(stages):
        copies = []
        for off in range(1, frames):
            dest = lax.rem(me + off, frames)
            copies.append(
                pltpu.make_async_remote_copy(
                    src_ref=qpart.at[pl.ds(lax.rem(dest + 1 + begin, frames), group)],
                    dst_ref=qrecv.at[off - 1, pl.ds(begin, group)],
                    send_sem=qsend_sem.at[off - 1, st],
                    recv_sem=qrecv_sem.at[off - 1, st],
                    device_id={"frame": dest},
                    device_id_type=MESH,
                )
            )
        queries.append(copies)
    for copy in queries[0]:
        copy.start()

    k = lax.broadcasted_iota(jnp.int32, (2 * LANES, LANES), 0)
    n = lax.broadcasted_iota(jnp.int32, (2 * LANES, LANES), 1)
    down = k // GRID_W - n // GRID_W
    along = k % GRID_W - n % GRID_W + 1
    inside = (down >= 0) & (down < 3) & (along >= 0) & (along < 3)
    tap = jnp.where(inside, 3 * down + along, -1)
    for i in (5, 6, 7):
        loads[i].wait()
    span = 2 * LANES
    for h in range(hid):
        band = jnp.zeros((span, LANES), F32)
        for j in range(9):
            band = jnp.where(tap == j, weight_ref[h : h + 1, j : j + 1], band)
        high = band.astype(BF16)
        at = slice((h % 2) * LANES, (h % 2 + 1) * LANES)
        bands[h // 2, :, at] = high
        bands8[h // 2, 0:span, at] = band.astype(F8)
        bands8[h // 2, span : 2 * span, at] = (band - high.astype(F32)).astype(F8)

    heads = [head_ref[0:1, h : h + 1] for h in range(hid)]
    floors = [-bias_ref[0:1, h : h + 1] for h in range(hid)]

    scale = 1.0 / math.sqrt(chan)

    for copies in queries[1:2]:
        for copy in copies:
            copy.start()
    sends = []

    def prepare(st):
        begin, group = stages[st]
        rows = group * sub
        xs, xs8 = xs_all.at[st % 2], xs8_all.at[st % 2]
        for held_in, base in ((xs, 0), (xs8, 0), (xs8, span)):
            blank = jnp.zeros((rows, GRID_W), held_in.dtype)
            held_in[0:rows, base : base + GRID_W] = blank
            held_in[(tiles - 1) * rows : tiles * rows, base + LANES + GRID_W : base + span] = blank
        q = qpart[pl.ds(lax.rem(me + 1 + begin, frames), group)].astype(F32)
        for off in range(1, frames):
            queries[st][off - 1].wait_recv()
            q = q + qrecv[off - 1, begin : begin + group].astype(F32)
        q = (q.reshape(rows, chan) * scale).astype(BF16)
        for copies in queries[st + 2 : st + 3]:
            for copy in copies:
                copy.start()

        for i in range(0, tiles + 1, 2):
            first = max(LANES * i - GRID_W, 0)
            last = min(LANES * (i + 2) - GRID_W, pixels)
            cost = lax.dot_general(
                q, maps_ref[first:last, :], (((1,), (1,)), ((), ())), preferred_element_type=F32
            )
            high = cost.astype(BF16)
            rest = (cost - high.astype(F32)).astype(F8)
            for out, base, value in ((xs, 0, high), (xs8, 0, rest), (xs8, span, cost.astype(F8))):
                if i == 0:
                    out[0:rows, base + GRID_W : base + LANES] = value[:, :GRID_W]
                    second = value[:, GRID_W : GRID_W + LANES]
                elif i == tiles:
                    out[(i - 1) * rows : i * rows, base + LANES : base + LANES + GRID_W] = value
                    continue
                else:
                    out[i * rows : (i + 1) * rows, base : base + LANES] = value[:, :LANES]
                    out[(i - 1) * rows : i * rows, base + LANES : base + span] = value[:, :LANES]
                    second = value[:, LANES:]
                out[i * rows : (i + 1) * rows, base + LANES : base + span] = second
                out[(i + 1) * rows : (i + 2) * rows, base : base + LANES] = second

    prepare(0)
    for st, (begin, group) in enumerate(stages):
        rows = group * sub
        xs, xs8, logit = xs_all.at[st % 2], xs8_all.at[st % 2], logit_all.at[st % 2]
        lane = lax.broadcasted_iota(jnp.int32, (rows, LANES), 1)
        low = (lane // GRID_W).astype(F32)
        colpos = (lane % GRID_W).astype(F32)
        chunk = min(256, tiles * rows)
        for start in range(0, tiles * rows, chunk):
            here = slice(start, start + chunk)
            left = xs[here, :]
            left8 = xs8[here, :]
            total_here = jnp.zeros((chunk, LANES), F32)
            for h in range(0, hid, 2):
                y = jnp.dot(left, bands[h // 2], preferred_element_type=F32)
                y = y + jnp.dot(left8, bands8[h // 2], preferred_element_type=F32)
                total_here = total_here + heads[h] * jnp.maximum(y[:, :LANES], floors[h])
                total_here = total_here + heads[h + 1] * jnp.maximum(y[:, LANES:], floors[h + 1])
            logit[here, :] = total_here

        if st + 1 < len(stages):
            prepare(st + 1)

        top = logit[0:rows, :]
        for i in range(1, tiles):
            top = jnp.maximum(top, logit[i * rows : (i + 1) * rows, :])
        top = jnp.max(top, axis=1, keepdims=True)
        mass = jnp.zeros((rows, LANES), F32)
        height = jnp.zeros((rows, LANES), F32)
        for i in range(tiles):
            e = jnp.exp(logit[i * rows : (i + 1) * rows, :] - top)
            logit[i * rows : (i + 1) * rows, :] = e
            mass = mass + e
            height = height + (2.0 * i) * e
        inv = 1.0 / jnp.sum(mass, axis=1, keepdims=True)
        row_est = jnp.sum(height + low * mass, axis=1, keepdims=True) * inv * (1.0 / (GRID_H - 1))
        col_est = jnp.sum(colpos * mass, axis=1, keepdims=True) * inv * (1.0 / (GRID_W - 1))
        sampled = jnp.zeros((rows, chan), F32)
        for i in range(0, tiles, 2):
            heat = jnp.concatenate(
                [
                    logit[i * rows : (i + 1) * rows, :] * inv,
                    logit[(i + 1) * rows : (i + 2) * rows, :] * inv,
                ],
                axis=1,
            ).astype(BF16)
            sampled = sampled + jnp.dot(
                heat, maps_ref[i * LANES : (i + 2) * LANES, :], preferred_element_type=F32
            )
        extra = jnp.where(lane == 0, row_est, jnp.where(lane == 1, col_est, 0.0))
        message = jnp.concatenate([sampled, extra], axis=1).astype(BF16).astype(wire)
        message = message.reshape(group, sub, chan + LANES)
        for g in range(group):
            j = begin + g
            if j == frames - 1:
                srecv[me] = message[g]
            else:
                ssend[j] = message[g]
                copy = pltpu.make_async_remote_copy(
                    src_ref=ssend.at[j],
                    dst_ref=srecv.at[me],
                    send_sem=ssend_sem.at[j],
                    recv_sem=srecv_sem.at[j],
                    device_id={"frame": lax.rem(me + 1 + j, frames)},
                    device_id_type=MESH,
                )
                copy.start()
                sends.append(copy)

    for j in range(frames - 1):
        sends[j].wait_recv()

    for i in (8, 9, 10, 11):
        loads[i].wait()
    got = srecv[...].astype(BF16) if wire != BF16 else srecv[...]
    rowcol = got[:, :, chan : chan + LANES].astype(F32)
    z = jnp.dot(
        got[:, :, :chan].reshape(slots_here, chan), mix_in_ref[...], preferred_element_type=F32
    )
    hidden = []
    for t in range(frames):
        mixed = taps_ref[1:2, :] * z[t * sub : (t + 1) * sub]
        if t > 0:
            mixed = taps_ref[0:1, :] * z[(t - 1) * sub : t * sub] + mixed
        if t < frames - 1:
            mixed = mixed + taps_ref[2:3, :] * z[(t + 1) * sub : (t + 2) * sub]
        mean = jnp.mean(mixed * mixed, axis=1, keepdims=True)
        normed = mixed * lax.rsqrt(mean + 1e-06) * gain_ref[...]
        hidden.append(jax.nn.gelu(normed).astype(BF16))
    delta = lax.dot_general(
        mix_out_ref[...],
        jnp.concatenate(hidden, axis=0),
        (((1,), (1,)), ((), ())),
        preferred_element_type=F32,
    )
    estimate = delta + rowcol.reshape(slots_here, LANES).T[0:3, :]
    for t in range(frames):
        for c in range(3):
            out_ref[c, t : t + 1, :] = estimate[c : c + 1, t * sub : (t + 1) * sub]

    for copy in [copy for copies in queries for copy in copies] + sends:
        copy.wait_send()


def on_device(
    feature_maps,
    query_frame,
    query_row,
    query_col,
    track_order,
    conv_weight,
    conv_bias,
    head_weight,
    mix_in,
    temporal_taps,
    mix_gain,
    mix_out,
):
    frames = lax.axis_size("frame")
    tracks = lax.axis_size("track")
    _, pixels, chan = feature_maps.shape
    total = track_order.shape[0]
    sub = total // (tracks * frames)
    hid = conv_weight.shape[0]
    mixw = mix_in.shape[1]
    wire = BF16 if sub % 16 == 0 else F32
    unit = max(1, min(frames, 32 // sub))
    cuts = sorted({0, unit, max(unit, frames - unit), frames})
    stages = [(begin, end - begin) for begin, end in zip(cuts, cuts[1:])]
    rows = sub * max(group for _, group in stages)
    tiles = pixels // LANES
    dma = pltpu.SemaphoreType.DMA
    args = (
        feature_maps.reshape(pixels, chan),
        query_frame.reshape(1, total),
        query_row.reshape(1, total),
        query_col.reshape(1, total),
        track_order.reshape(1, total),
        conv_weight,
        conv_bias.reshape(1, hid),
        head_weight.reshape(1, hid),
        mix_in,
        temporal_taps,
        mix_gain.reshape(1, mixw),
        mix_out.T,
    )
    out = pl.pallas_call(
        functools.partial(kernel, (frames, tracks, sub, stages, wire)),
        out_shape=pltpu.VMEM((3, frames, sub), F32),
        in_specs=[pl.BlockSpec(memory_space=pl.ANY)] * len(args),
        out_specs=pl.BlockSpec(memory_space=pltpu.VMEM),
        scratch_shapes=[pltpu.VMEM(x.shape, x.dtype) for x in args]
        + [
            pltpu.VMEM((2 * frames, sub, chan), wire),
            pltpu.VMEM((frames - 1, frames, sub, chan), wire),
            pltpu.VMEM((2, tiles * rows, 2 * LANES), BF16),
            pltpu.VMEM((2, tiles * rows, 4 * LANES), F8),
            pltpu.VMEM((hid // 2, 2 * LANES, 2 * LANES), BF16),
            pltpu.VMEM((hid // 2, 4 * LANES, 2 * LANES), F8),
            pltpu.VMEM((2, tiles * rows, LANES), F32),
            pltpu.VMEM((frames - 1, sub, chan + LANES), wire),
            pltpu.VMEM((frames, sub, chan + LANES), wire),
            dma((frames - 1, len(stages))),
            dma((frames - 1, len(stages))),
            dma((frames - 1,)),
            dma((frames - 1,)),
            dma((len(args),)),
            dma((4,)),
        ],
        compiler_params=pltpu.CompilerParams(
            collective_id=0, has_side_effects=True, vmem_limit_bytes=56 * 1024 * 1024
        ),
    )(*args)
    return out.transpose(2, 0, 1)


def solution(mesh):
    placed = (
        P(("clip", "frame"), None, None),
        P("clip"),
        P("clip"),
        P("clip"),
        P("clip"),
        P(),
        P(),
        P(),
        P(),
        P(),
        P(),
        P(),
    )
    return jax.shard_map(
        on_device,
        mesh=mesh,
        in_specs=placed,
        out_specs=P(("clip", "frame", "track"), None, None),
        check_vma=False,
    )
```
